32 devices in a mesh: node: 4 (over z), cuts: 8 (over y, x, core).
Axes of the slice: x: 2, y: 2, z: 4, core: 2. Of those that a mesh axis runs over, the one named last changes fastest.
Arguments:
- core_x: bfloat16 [8, 256, 256, 256], P('node', 'cuts'), may hold values from -6 to 6
- core_y: bfloat16 [8, 256, 256, 256], P('node', 'cuts'), may hold values from -0.0234375 to 0.0234375
- left_intersection: bfloat16 [8, 256, 256], P('node', 'cuts'), may hold values from -0.375 to 0.375
- right_intersection: bfloat16 [8, 256, 256], P('node', 'cuts'), may hold values from -0.375 to 0.375
Outputs:
- parent_intersection: float32 [8, 256, 256], P('node', 'cuts')
The draws below stay inside these ranges and needn't reach their ends.
All inputs are finite; a program needn't handle non-finite values.
Results may differ from the reference program's by a relative error of at most 0.004.
Values may be sent and summed in bfloat16 or wider, within the bound.
No kernel may reach another device: no remote copies, remote signals or barrier semaphores. Data moves between devices by JAX's collectives and lax.ppermute only.
A program may use at most 64 MiB of HBM per device.

```python
import jax
import jax.numpy as jnp
from jax import lax

R = 256
PARENTS = 8


def block_scale(stream_key, shape, shards, low, high):
    gain, own = 1.0, jax.random.fold_in(stream_key, 6)
    for position, blocks in shards:
        steps = jnp.exp(jax.random.uniform(jax.random.fold_in(own, position), (blocks,), jnp.float32, low / len(shards), high / len(shards)))
        gain = gain * jnp.repeat(steps, shape[position] // blocks).reshape([-1 if axis == position else 1 for axis in range(len(shape))])
    return gain


def gaussian(own_key, extent, deviation, reach, pieces=(), dtype=jnp.bfloat16):
    values = deviation * jax.random.normal(own_key, extent, jnp.float32)
    if pieces:
        values = values * block_scale(own_key, extent, pieces, -0.22, 0.18)
    return jnp.clip(values, -reach, reach).astype(dtype)


def setup_inputs(seed: int = 0) -> dict:
    streams_of = jax.random.split(jax.random.key(seed), 5)
    return {
        "core_x": gaussian(streams_of[0], (PARENTS, R, R, R), 1.0, 6.0, ((0, 4), (1, 8))),
        "core_y": gaussian(streams_of[1], (PARENTS, R, R, R), (R * R) ** -0.5, 0.0234375, ((0, 4), (1, 8))),
        "left_intersection": gaussian(streams_of[2], (PARENTS, R, R), R ** -0.5, 0.375, ((0, 4), (1, 8))),
        "right_intersection": gaussian(streams_of[3], (PARENTS, R, R), R ** -0.5, 0.375, ((0, 4), (1, 8))),
    }


def one_parent(items):
    block_x, block_y, left_mat, right_mat = items
    first = jnp.einsum("ik,aij->akj", left_mat.astype(jnp.float32), block_x.astype(jnp.float32)).astype(jnp.bfloat16)
    second = jnp.einsum("akj,jl->akl", first.astype(jnp.float32), right_mat.astype(jnp.float32)).astype(jnp.bfloat16)
    return jnp.einsum("akl,klb->ab", second.astype(jnp.float32), block_y.astype(jnp.float32))


def reference(core_x, core_y, left_intersection, right_intersection):
    return lax.map(one_parent, (core_x, core_y, left_intersection, right_intersection))
```

```python
import functools

import jax
import jax.numpy as jnp
from jax import lax
from jax.experimental import pallas as pl
from jax.experimental.pallas import tpu as pltpu
from jax.sharding import PartitionSpec as P

AXIS = "cuts"
LIMIT = 48 * 1024 * 1024
LANES = 128


def plain(core_x, core_y, left_intersection, right_intersection):
    left_full = lax.all_gather(left_intersection, AXIS, axis=1, tiled=True)
    first = jnp.einsum(
        "pik,paij->pakj", left_full, core_x, preferred_element_type=jnp.float32
    ).astype(jnp.bfloat16)
    right_full = lax.all_gather(right_intersection, AXIS, axis=1, tiled=True)
    moved = lax.all_to_all(
        jnp.einsum("pakj,pjl->pakl", first, right_full, preferred_element_type=jnp.float32).astype(
            jnp.bfloat16
        ),
        AXIS,
        split_axis=2,
        concat_axis=1,
        tiled=True,
    )
    mine = lax.psum_scatter(
        jnp.einsum("pakl,pklb->apb", moved, core_y, preferred_element_type=jnp.float32),
        AXIS,
        scatter_dimension=0,
        tiled=True,
    )
    return jnp.transpose(mine, (1, 0, 2))


def swap(value, mask, n):
    return lax.ppermute(value, AXIS, [(i, i ^ mask) for i in range(n)])


def gather_rows(value, n):
    rows = [None] * n
    rows[0] = value
    for mask in range(n - 2, 0, -2):
        rows[mask] = swap(value, mask, n)
    for mask in range(0, n, 2):
        rows[mask + 1] = swap(rows[mask], 1, n)
    return rows


def first_kernel(n, masks, me_ref, *refs):
    pieces, x_ref = refs[:n], refs[n]
    outs, (full, turned, chosen) = refs[n + 1 : n + 1 + len(masks)], refs[n + 1 + len(masks) :]
    rows = pieces[0].shape[1]
    me = me_ref[0]

    @pl.when(pl.program_id(1) == 0)
    def _():
        for m in range(n):
            full[pl.ds(pl.multiple_of((me ^ m) * rows, rows), rows), :] = pieces[m][0]
        turned[...] = full[...].T
        for slot, m in enumerate(masks):
            chosen[slot * rows : (slot + 1) * rows, :] = turned[
                pl.ds(pl.multiple_of((me ^ m) * rows, rows), rows), :
            ]

    for a in range(x_ref.shape[1]):
        product = jnp.dot(chosen[...], x_ref[0, a], preferred_element_type=jnp.float32).astype(jnp.bfloat16)
        for slot, out in enumerate(outs):
            out[0, a] = product[slot * rows : (slot + 1) * rows, :]


def first_for(me, pieces, core_x, masks):
    n = len(pieces)
    parents, mine, left, right = core_x.shape
    rows = pieces[0].shape[1]
    step = min(8, mine)
    spec = pl.BlockSpec((1, rows, left), lambda p, c: (p, 0, 0))
    return pl.pallas_call(
        functools.partial(first_kernel, n, masks),
        grid=(parents, mine // step),
        in_specs=[pl.BlockSpec(memory_space=pltpu.SMEM)]
        + [spec] * n
        + [pl.BlockSpec((1, step, left, right), lambda p, c: (p, c, 0, 0))],
        out_specs=[pl.BlockSpec((1, step, rows, right), lambda p, c: (p, c, 0, 0))] * len(masks),
        out_shape=[jax.ShapeDtypeStruct((parents, mine, rows, right), jnp.bfloat16)] * len(masks),
        scratch_shapes=[
            pltpu.VMEM((left, left), jnp.bfloat16),
            pltpu.VMEM((left, left), jnp.bfloat16),
            pltpu.VMEM((rows * len(masks), left), jnp.bfloat16),
        ],
        compiler_params=pltpu.CompilerParams(vmem_limit_bytes=LIMIT),
        cost_estimate=pl.CostEstimate(
            flops=2 * parents * mine * rows * len(masks) * left * right,
            bytes_accessed=2 * parents * mine * right * (left + rows * len(masks)),
            transcendentals=0,
        ),
        name="first",
    )(me, *pieces, core_x)


def join_kernel(n, me_ref, *refs):
    pieces, out = refs[:n], refs[n]
    rows = pieces[0].shape[1]
    for m in range(n):
        at = pl.ds(pl.multiple_of((me_ref[0] ^ m) * rows, rows), rows)
        out[:, at, :] = pieces[m][...]


def join(me, pieces):
    n = len(pieces)
    parents, rows, width = pieces[0].shape
    return pl.pallas_call(
        functools.partial(join_kernel, n),
        in_specs=[pl.BlockSpec(memory_space=pltpu.SMEM)] + [pl.BlockSpec(memory_space=pltpu.VMEM)] * n,
        out_specs=pl.BlockSpec(memory_space=pltpu.VMEM),
        out_shape=jax.ShapeDtypeStruct((parents, n * rows, width), pieces[0].dtype),
        cost_estimate=pl.CostEstimate(flops=0, bytes_accessed=4 * parents * n * rows * width, transcendentals=0),
        name="join",
    )(me, *pieces)


def last_kernel(held, first_ref, right_ref, y_ref, *refs):
    out_ref, second, flat = refs[-3:]
    count, rows = first_ref.shape[1], first_ref.shape[2]
    width = right_ref.shape[2]
    c = pl.program_id(1)

    @pl.when(c == 0)
    def _():
        whole = jnp.dot(
            first_ref[0].reshape(count * rows, first_ref.shape[3]),
            right_ref[0],
            preferred_element_type=jnp.float32,
        )
        for h in range(width // LANES):
            second[h] = whole[:, h * LANES : (h + 1) * LANES]
        for k in range(rows):
            for h in range(width // LANES):
                flat[:, k * width + h * LANES : k * width + (h + 1) * LANES] = second[
                    h, pl.ds(k, count, stride=rows), :
                ].astype(jnp.bfloat16)
        if held:
            out_ref[...] = refs[0][...]
        else:
            out_ref[...] = jnp.zeros_like(out_ref)

    depth = y_ref.shape[1] * width
    out_ref[0] += jnp.dot(
        flat[:, pl.ds(pl.multiple_of(c * depth, depth), depth)],
        y_ref[0].reshape(depth, y_ref.shape[3]),
        preferred_element_type=jnp.float32,
    )


def last_for(first, right_full, core_y, begin=None):
    parents, count, rows, depth = first.shape
    width, out_width = right_full.shape[2], core_y.shape[3]
    step = min(8, rows)
    spec = pl.BlockSpec((1, count, out_width), lambda p, c: (p, 0, 0))
    return pl.pallas_call(
        functools.partial(last_kernel, begin is not None),
        grid=(parents, rows // step),
        in_specs=[
            pl.BlockSpec((1, count, rows, depth), lambda p, c: (p, 0, 0, 0)),
            pl.BlockSpec((1, depth, width), lambda p, c: (p, 0, 0)),
            pl.BlockSpec((1, step, width, out_width), lambda p, c: (p, c, 0, 0)),
        ]
        + [spec] * (begin is not None),
        out_specs=spec,
        out_shape=jax.ShapeDtypeStruct((parents, count, out_width), jnp.float32),
        scratch_shapes=[
            pltpu.VMEM((width // LANES, count * rows, LANES), jnp.float32),
            pltpu.VMEM((count, rows * width), jnp.bfloat16),
        ],
        compiler_params=pltpu.CompilerParams(vmem_limit_bytes=LIMIT),
        cost_estimate=pl.CostEstimate(
            flops=2 * parents * count * rows * width * (depth + out_width),
            bytes_accessed=2 * parents * rows * width * (count + out_width),
            transcendentals=0,
        ),
        name="last",
    )(first, right_full, core_y, *([] if begin is None else [begin]))


def exchanged(core_x, core_y, left_intersection, right_intersection, n):
    me = lax.axis_index(AXIS).astype(jnp.int32).reshape(1)
    pairs = list(range(2, n, 2))
    left = gather_rows(left_intersection, n)
    early = [mask + 1 for mask in pairs[:2]]
    late = [mask for mask in range(n) if mask not in early]
    sent = dict(zip(early, first_for(me, left, core_x, early)))
    came = {mask: swap(sent[mask], mask, n) for mask in early}
    sent.update(zip(late, first_for(me, left, core_x, late)))
    for mask in [m for m in pairs[:2]] + [m + 1 for m in pairs[2:]] + pairs[2:] + [1]:
        came[mask] = swap(sent[mask], mask, n)
    came[0] = sent[0]
    right = join(me, gather_rows(right_intersection, n))
    total = []
    for mask in pairs + [0]:
        odd = last_for(came[mask + 1], right, core_y)
        part = last_for(came[mask], right, core_y, swap(odd, 1, n))
        total.append(swap(part, mask, n) if mask else part)
    return sum(total[1:], total[0])


def solution(mesh):
    n = mesh.shape[AXIS]

    def shards(core_x, core_y, left_intersection, right_intersection):
        rows = left_intersection.shape[1]
        fits = n >= 4 and n & (n - 1) == 0 and rows % 16 == 0 and core_x.shape[1] % 8 == 0 and core_x.shape[3] % LANES == 0
        if not fits:
            return plain(core_x, core_y, left_intersection, right_intersection)
        return exchanged(core_x, core_y, left_intersection, right_intersection, n)

    return jax.shard_map(
        shards,
        mesh=mesh,
        in_specs=(
            P("node", AXIS, None, None),
            P("node", AXIS, None, None),
            P("node", AXIS, None),
            P("node", AXIS, None),
        ),
        out_specs=P("node", AXIS, None),
        check_vma=False,
    )
```

```python
import functools

import jax
import jax.numpy as jnp
from jax import lax
from jax.experimental import pallas as pl
from jax.experimental.pallas import tpu as pltpu
from jax.sharding import PartitionSpec as P

AXIS = "cuts"
LIMIT = 20 * 1024 * 1024
LANES = 128


def plain(core_x, core_y, left_intersection, right_intersection):
    left_full = lax.all_gather(left_intersection, AXIS, axis=1, tiled=True)
    first = jnp.einsum(
        "pik,paij->pakj", left_full, core_x, preferred_element_type=jnp.float32
    ).astype(jnp.bfloat16)
    right_full = lax.all_gather(right_intersection, AXIS, axis=1, tiled=True)
    moved = lax.all_to_all(
        jnp.einsum("pakj,pjl->pakl", first, right_full, preferred_element_type=jnp.float32).astype(
            jnp.bfloat16
        ),
        AXIS,
        split_axis=2,
        concat_axis=1,
        tiled=True,
    )
    mine = lax.psum_scatter(
        jnp.einsum("pakl,pklb->apb", moved, core_y, preferred_element_type=jnp.float32),
        AXIS,
        scatter_dimension=0,
        tiled=True,
    )
    return jnp.transpose(mine, (1, 0, 2))


def swap(value, mask, n):
    return lax.ppermute(value, AXIS, [(i, i ^ mask) for i in range(n)])


def off_chip_rows(value, n):
    return {mask: swap(value, mask, n) if mask else value for mask in range(n - 2, -2, -2)}


def both_cores(even, n):
    rows = [None] * n
    for mask, value in even.items():
        rows[mask], rows[mask + 1] = value, swap(value, 1, n)
    return rows


def first_kernel(n, masks, me_ref, *refs):
    pieces, x_ref = refs[:n], refs[n]
    outs, (full, turned, chosen) = refs[-3 - len(masks) : -3], refs[-3:]
    rows = pieces[0].shape[1]
    parent, chunk, step = pl.program_id(0), pl.program_id(1), outs[0].shape[1]
    me = me_ref[0]

    @pl.when(chunk == 0)
    def _():
        for m in range(n):
            full[pl.ds(pl.multiple_of((me ^ m) * rows, rows), rows), :] = pieces[m][0]
        turned[...] = full[...].T
        for slot, m in enumerate(masks):
            chosen[slot * rows : (slot + 1) * rows, :] = turned[
                pl.ds(pl.multiple_of((me ^ m) * rows, rows), rows), :
            ]

    for a in range(step):
        product = jnp.dot(
            chosen[...], x_ref[parent, chunk * step + a], preferred_element_type=jnp.float32
        ).astype(jnp.bfloat16)
        for slot, out in enumerate(outs):
            out[0, a] = product[slot * rows : (slot + 1) * rows, :]


def first_for(me, pieces, core_x, masks, after=()):
    n = len(pieces)
    parents, mine, left, right = core_x.shape
    rows = pieces[0].shape[1]
    step = min(8, mine)
    spec = pl.BlockSpec((1, rows, left), lambda p, c: (p, 0, 0))
    return pl.pallas_call(
        functools.partial(first_kernel, n, masks),
        grid=(parents, mine // step),
        in_specs=[pl.BlockSpec(memory_space=pltpu.SMEM)]
        + [spec] * n
        + [pl.BlockSpec(memory_space=pltpu.VMEM)]
        + [pl.BlockSpec(memory_space=pl.ANY)] * len(after),
        out_specs=[pl.BlockSpec((1, step, rows, right), lambda p, c: (p, c, 0, 0))] * len(masks),
        out_shape=[jax.ShapeDtypeStruct((parents, mine, rows, right), jnp.bfloat16)] * len(masks),
        scratch_shapes=[
            pltpu.VMEM((left, left), jnp.bfloat16),
            pltpu.VMEM((left, left), jnp.bfloat16),
            pltpu.VMEM((rows * len(masks), left), jnp.bfloat16),
        ],
        compiler_params=pltpu.CompilerParams(vmem_limit_bytes=LIMIT),
        cost_estimate=pl.CostEstimate(
            flops=2 * parents * mine * rows * len(masks) * left * right,
            bytes_accessed=2 * parents * mine * right * (left + rows * len(masks)),
            transcendentals=0,
        ),
        name="first",
    )(me, *pieces, core_x, *after)


def join_kernel(n, me_ref, *refs):
    pieces, out = refs[:n], refs[n]
    rows = pieces[0].shape[1]
    for m in range(n):
        at = pl.ds(pl.multiple_of((me_ref[0] ^ m) * rows, rows), rows)
        out[:, at, :] = pieces[m][...]


def join(me, pieces):
    n = len(pieces)
    parents, rows, width = pieces[0].shape
    return pl.pallas_call(
        functools.partial(join_kernel, n),
        in_specs=[pl.BlockSpec(memory_space=pltpu.SMEM)] + [pl.BlockSpec(memory_space=pltpu.VMEM)] * n,
        out_specs=pl.BlockSpec(memory_space=pltpu.VMEM),
        out_shape=jax.ShapeDtypeStruct((parents, n * rows, width), pieces[0].dtype),
        cost_estimate=pl.CostEstimate(flops=0, bytes_accessed=4 * parents * n * rows * width, transcendentals=0),
        name="join",
    )(me, *pieces)


def last_kernel(held, first_ref, right_ref, y_ref, *refs):
    out_ref, second, flat = refs[-3:]
    count, rows = first_ref.shape[1], first_ref.shape[2]
    width = right_ref.shape[2]
    whole = jnp.dot(
        first_ref[0].reshape(count * rows, first_ref.shape[3]),
        right_ref[0],
        preferred_element_type=jnp.float32,
    )
    for h in range(width // LANES):
        second[h] = whole[:, h * LANES : (h + 1) * LANES]
    for k in range(rows):
        for h in range(width // LANES):
            flat[:, k * width + h * LANES : k * width + (h + 1) * LANES] = second[
                h, pl.ds(k, count, stride=rows), :
            ].astype(jnp.bfloat16)
    total = jnp.dot(
        flat[...],
        y_ref[pl.program_id(0)].reshape(rows * width, y_ref.shape[3]),
        preferred_element_type=jnp.float32,
    )
    out_ref[0] = total + refs[0][0] if held else total


def last_for(first, right_full, core_y, begin=None):
    parents, count, rows, depth = first.shape
    width, out_width = right_full.shape[2], core_y.shape[3]
    spec = pl.BlockSpec((1, count, out_width), lambda p: (p, 0, 0))
    return pl.pallas_call(
        functools.partial(last_kernel, begin is not None),
        grid=(parents,),
        in_specs=[
            pl.BlockSpec((1, count, rows, depth), lambda p: (p, 0, 0, 0)),
            pl.BlockSpec((1, depth, width), lambda p: (p, 0, 0)),
            pl.BlockSpec(memory_space=pltpu.VMEM),
        ]
        + [spec] * (begin is not None),
        out_specs=spec,
        out_shape=jax.ShapeDtypeStruct((parents, count, out_width), jnp.float32),
        scratch_shapes=[
            pltpu.VMEM((width // LANES, count * rows, LANES), jnp.float32),
            pltpu.VMEM((count, rows * width), jnp.bfloat16),
        ],
        compiler_params=pltpu.CompilerParams(vmem_limit_bytes=LIMIT),
        cost_estimate=pl.CostEstimate(
            flops=2 * parents * count * rows * width * (depth + out_width),
            bytes_accessed=2 * parents * rows * width * (count + out_width),
            transcendentals=0,
        ),
        name="last",
    )(first, right_full, core_y, *([] if begin is None else [begin]))


def exchanged(core_x, core_y, left_intersection, right_intersection, n):
    me = lax.axis_index(AXIS).astype(jnp.int32).reshape(1)
    pairs = list(range(2, n, 2))
    left = off_chip_rows(left_intersection, n)
    right = off_chip_rows(right_intersection, n)
    left = both_cores(left, n)
    early = [mask + 1 for mask in pairs[:2]]
    late = [mask for mask in range(n) if mask not in early]
    sent = dict(zip(early, first_for(me, left, core_x, early, list(right.values()))))
    came = {mask: swap(sent[mask], mask, n) for mask in early}
    sent.update(zip(late, first_for(me, left, core_x, late)))
    for mask in [m for m in pairs[:2]] + [m + 1 for m in pairs[2:]] + pairs[2:] + [1]:
        came[mask] = swap(sent[mask], mask, n)
    came[0] = sent[0]
    right = join(me, both_cores(right, n))
    total = []
    for mask in pairs + [0]:
        odd = last_for(came[mask + 1], right, core_y)
        part = last_for(came[mask], right, core_y, swap(odd, 1, n))
        total.append(swap(part, mask, n) if mask else part)
    return sum(total[1:], total[0])


def solution(mesh):
    n = mesh.shape[AXIS]

    def shards(core_x, core_y, left_intersection, right_intersection):
        rows = left_intersection.shape[1]
        fits = n >= 4 and n & (n - 1) == 0 and rows % 16 == 0 and core_x.shape[1] % 8 == 0 and core_x.shape[3] % LANES == 0
        if not fits:
            return plain(core_x, core_y, left_intersection, right_intersection)
        return exchanged(core_x, core_y, left_intersection, right_intersection, n)

    return jax.shard_map(
        shards,
        mesh=mesh,
        in_specs=(
            P("node", AXIS, None, None),
            P("node", AXIS, None, None),
            P("node", AXIS, None),
            P("node", AXIS, None),
        ),
        out_specs=P("node", AXIS, None),
        check_vma=False,
    )
```

```python
import functools

import jax
import jax.numpy as jnp
from jax import lax
from jax.experimental import pallas as pl
from jax.experimental.pallas import tpu as pltpu
from jax.sharding import PartitionSpec as P

AXIS = "cuts"
LIMIT = 20 * 1024 * 1024
LANES = 128


def plain(core_x, core_y, left_intersection, right_intersection):
    left_full = lax.all_gather(left_intersection, AXIS, axis=1, tiled=True)
    first = jnp.einsum(
        "pik,paij->pakj", left_full, core_x, preferred_element_type=jnp.float32
    ).astype(jnp.bfloat16)
    right_full = lax.all_gather(right_intersection, AXIS, axis=1, tiled=True)
    moved = lax.all_to_all(
        jnp.einsum("pakj,pjl->pakl", first, right_full, preferred_element_type=jnp.float32).astype(
            jnp.bfloat16
        ),
        AXIS,
        split_axis=2,
        concat_axis=1,
        tiled=True,
    )
    mine = lax.psum_scatter(
        jnp.einsum("pakl,pklb->apb", moved, core_y, preferred_element_type=jnp.float32),
        AXIS,
        scatter_dimension=0,
        tiled=True,
    )
    return jnp.transpose(mine, (1, 0, 2))


def swap(value, mask, n):
    return lax.ppermute(value, AXIS, [(i, i ^ mask) for i in range(n)])


def gather_rows(value, n):
    even = {mask: swap(value, mask, n) for mask in range(n - 2, 0, -2)}
    even[0] = value
    rows = [None] * n
    for mask, came in even.items():
        rows[mask], rows[mask + 1] = came, swap(came, 1, n)
    return rows


def stage_kernel(x_ref, out_ref, sems):
    parents, count = sems.shape
    step = x_ref.shape[1] // count
    copies = [
        pltpu.make_async_copy(
            x_ref.at[p, pl.ds(c * step, step)], out_ref.at[p, pl.ds(c * step, step)], sems.at[p, c]
        )
        for p in range(parents)
        for c in range(count)
    ]
    for copy in copies:
        copy.start()
    for copy in copies:
        copy.wait()


def staged(core):
    return pl.pallas_call(
        stage_kernel,
        in_specs=[pl.BlockSpec(memory_space=pl.ANY)],
        out_specs=pl.BlockSpec(memory_space=pl.ANY),
        out_shape=jax.ShapeDtypeStruct(core.shape, core.dtype),
        scratch_shapes=[pltpu.SemaphoreType.DMA((core.shape[0], 4))],
        compiler_params=pltpu.CompilerParams(vmem_limit_bytes=LIMIT),
        cost_estimate=pl.CostEstimate(flops=0, bytes_accessed=4 * core.size, transcendentals=0),
        name="stage",
    )(core)


def at_rows(me, mask, rows):
    return pl.ds(pl.multiple_of((me ^ mask) * rows, rows), rows)


def choose(me, masks, pieces, full, turned, chosen):
    rows = chosen.shape[0] // len(masks)
    for m, piece in enumerate(pieces):
        full[at_rows(me, m, rows), :] = piece[0, :rows]
    turned[...] = full[...].T
    for slot, m in enumerate(masks):
        chosen[slot * rows : (slot + 1) * rows, :] = turned[at_rows(me, m, rows), :]


def apply_right(first, right, second, flat_ref, count, rows):
    width = right.shape[1]
    whole = jnp.dot(first, right, preferred_element_type=jnp.float32)
    for h in range(width // LANES):
        second[h] = whole[:, h * LANES : (h + 1) * LANES]
    for k in range(rows):
        for h in range(width // LANES):
            flat_ref[:, k * width + h * LANES : k * width + (h + 1) * LANES] = second[
                h, pl.ds(k, count, stride=rows), :
            ].astype(jnp.bfloat16)


def first_kernel(n, masks, me_ref, *refs):
    pieces, x_ref = refs[:n], refs[n]
    outs, (full, turned, chosen) = refs[n + 1 : n + 1 + len(masks)], refs[-3:]
    parent, chunk = pl.program_id(0), pl.program_id(1)
    step, rows = outs[0].shape[1], outs[0].shape[2]

    @pl.when(chunk == 0)
    def _():
        choose(me_ref[0], masks, pieces, full, turned, chosen)

    for a in range(step):
        product = jnp.dot(
            chosen[...], x_ref[parent, chunk * step + a], preferred_element_type=jnp.float32
        ).astype(jnp.bfloat16)
        for slot, out in enumerate(outs):
            out[0, a] = product[slot * rows : (slot + 1) * rows, :]


def first_for(me, pieces, core_x, masks):
    n = len(pieces)
    parents, mine, left, right = core_x.shape
    rows = left // n
    step = min(8, mine)
    return pl.pallas_call(
        functools.partial(first_kernel, n, masks),
        grid=(parents, mine // step),
        in_specs=[pl.BlockSpec(memory_space=pltpu.SMEM)]
        + [pl.BlockSpec((1, 2 * rows, left), lambda p, c: (p, 0, 0))] * n
        + [pl.BlockSpec(memory_space=pltpu.VMEM)],
        out_specs=[pl.BlockSpec((1, step, rows, right), lambda p, c: (p, c, 0, 0))] * len(masks),
        out_shape=[jax.ShapeDtypeStruct((parents, mine, rows, right), jnp.bfloat16)] * len(masks),
        scratch_shapes=[
            pltpu.VMEM((left, left), jnp.bfloat16),
            pltpu.VMEM((left, left), jnp.bfloat16),
            pltpu.VMEM((rows * len(masks), left), jnp.bfloat16),
        ],
        compiler_params=pltpu.CompilerParams(vmem_limit_bytes=LIMIT),
        cost_estimate=pl.CostEstimate(
            flops=2 * parents * mine * rows * len(masks) * left * right,
            bytes_accessed=2 * parents * mine * right * (left + rows * len(masks)),
            transcendentals=0,
        ),
        name="first",
    )(me, *pieces, core_x)


def second_kernel(n, masks, me_ref, *refs):
    pieces, x_ref = refs[:n], refs[n]
    outs, (full, turned, chosen, first, second) = refs[-5 - len(masks) : -5], refs[-5:]
    parent = pl.program_id(0)
    mine, rows = outs[0].shape[1], pieces[0].shape[1] // 2
    choose(me_ref[0], masks, pieces, full, turned, chosen)
    for m, piece in enumerate(pieces):
        full[at_rows(me_ref[0], m, rows), :] = piece[0, rows:]
    for a in range(mine):
        product = jnp.dot(chosen[...], x_ref[parent, a], preferred_element_type=jnp.float32).astype(jnp.bfloat16)
        for slot in range(len(masks)):
            first[slot, a * rows : (a + 1) * rows, :] = product[slot * rows : (slot + 1) * rows, :]
    for slot, out in enumerate(outs):
        apply_right(first[slot], full[...], second, out.at[0], mine, rows)


def second_for(me, pieces, core_x, masks, after):
    n = len(pieces)
    parents, mine, left, right = core_x.shape
    rows = left // n
    return pl.pallas_call(
        functools.partial(second_kernel, n, masks),
        grid=(parents,),
        in_specs=[pl.BlockSpec(memory_space=pltpu.SMEM)]
        + [pl.BlockSpec((1, 2 * rows, left), lambda p: (p, 0, 0))] * n
        + [pl.BlockSpec(memory_space=pltpu.VMEM), pl.BlockSpec(memory_space=pl.ANY)],
        out_specs=[pl.BlockSpec((1, mine, rows * right), lambda p: (p, 0, 0))] * len(masks),
        out_shape=[jax.ShapeDtypeStruct((parents, mine, rows * right), jnp.bfloat16)] * len(masks),
        scratch_shapes=[
            pltpu.VMEM((left, left), jnp.bfloat16),
            pltpu.VMEM((left, left), jnp.bfloat16),
            pltpu.VMEM((rows * len(masks), left), jnp.bfloat16),
            pltpu.VMEM((len(masks), mine * rows, right), jnp.bfloat16),
            pltpu.VMEM((right // LANES, mine * rows, LANES), jnp.float32),
        ],
        compiler_params=pltpu.CompilerParams(vmem_limit_bytes=LIMIT),
        cost_estimate=pl.CostEstimate(
            flops=2 * parents * mine * rows * len(masks) * right * (left + right),
            bytes_accessed=2 * parents * mine * right * (left + rows * len(masks)),
            transcendentals=0,
        ),
        name="second",
    )(me, *pieces, core_x, after)


def join_kernel(n, me_ref, *refs):
    pieces, out = refs[:n], refs[n]
    rows = pieces[0].shape[1] // 2
    for m in range(n):
        out[:, at_rows(me_ref[0], m, rows), :] = pieces[m][:, rows:]


def join_right(me, pieces):
    n = len(pieces)
    parents, rows, width = pieces[0].shape
    return pl.pallas_call(
        functools.partial(join_kernel, n),
        in_specs=[pl.BlockSpec(memory_space=pltpu.SMEM)] + [pl.BlockSpec(memory_space=pltpu.VMEM)] * n,
        out_specs=pl.BlockSpec(memory_space=pltpu.VMEM),
        out_shape=jax.ShapeDtypeStruct((parents, n * rows // 2, width), pieces[0].dtype),
        compiler_params=pltpu.CompilerParams(vmem_limit_bytes=LIMIT),
        cost_estimate=pl.CostEstimate(flops=0, bytes_accessed=2 * parents * n * rows * width, transcendentals=0),
        name="join",
    )(me, *pieces)


def last_kernel(held, right_given, came_ref, y_ref, *refs):
    begin_ref = refs[0] if held else None
    parent = pl.program_id(0)
    depth = y_ref.shape[1] * y_ref.shape[2]
    if right_given:
        right_ref, out_ref, second, flat = refs[-4:]
        count, rows = came_ref.shape[1], came_ref.shape[2]
        apply_right(
            came_ref[0].reshape(count * rows, came_ref.shape[3]), right_ref[0], second, flat, count, rows
        )
        wide = flat[...]
    else:
        out_ref = refs[-1]
        wide = came_ref[0]
    total = jnp.dot(wide, y_ref[parent].reshape(depth, y_ref.shape[3]), preferred_element_type=jnp.float32)
    out_ref[0] = total + begin_ref[0] if held else total


def last_for(came, core_y, begin=None, right=None):
    parents, rows, width, out_width = core_y.shape
    count = came.shape[1]
    row = pl.BlockSpec((1, count, out_width), lambda p: (p, 0, 0))
    zeros = (0,) * (came.ndim - 1)
    given = [came, core_y]
    specs = [
        pl.BlockSpec((1,) + came.shape[1:], lambda p: (p,) + zeros),
        pl.BlockSpec(memory_space=pltpu.VMEM),
    ]
    scratch = []
    if begin is not None:
        given, specs = given + [begin], specs + [row]
    if right is not None:
        given, specs = given + [right], specs + [pl.BlockSpec((1,) + right.shape[1:], lambda p: (p, 0, 0))]
        scratch = [
            pltpu.VMEM((width // LANES, count * rows, LANES), jnp.float32),
            pltpu.VMEM((count, rows * width), jnp.bfloat16),
        ]
    return pl.pallas_call(
        functools.partial(last_kernel, begin is not None, right is not None),
        grid=(parents,),
        in_specs=specs,
        out_specs=row,
        out_shape=jax.ShapeDtypeStruct((parents, count, out_width), jnp.float32),
        scratch_shapes=scratch,
        compiler_params=pltpu.CompilerParams(vmem_limit_bytes=LIMIT),
        cost_estimate=pl.CostEstimate(
            flops=2 * parents * count * rows * width * (out_width + (width if scratch else 0)),
            bytes_accessed=2 * parents * rows * width * (count + out_width),
            transcendentals=0,
        ),
        name="last",
    )(*given)


def exchanged(core_x, core_y, left_intersection, right_intersection, n):
    me = lax.axis_index(AXIS).astype(jnp.int32).reshape(1)
    pairs = list(range(2, n, 2))
    pieces = gather_rows(jnp.concatenate([left_intersection, right_intersection], axis=1), n)
    core_x = staged(core_x)
    early = [mask + 1 for mask in pairs[:2]]
    sent = dict(zip(early, first_for(me, pieces, core_x, early)))
    came = {mask: swap(sent[mask], mask, n) for mask in early}
    after = sent[early[0]]
    for masks in [pairs[:2]] + [[mask + 1, mask] for mask in pairs[2:]] + [[1, 0]]:
        sent.update(zip(masks, second_for(me, pieces, core_x, masks, after)))
        after = sent[masks[0]]
        for mask in masks:
            came[mask] = swap(sent[mask], mask, n) if mask else sent[0]
    right = join_right(me, pieces)
    total = []
    for mask in pairs + [0]:
        odd = last_for(came[mask + 1], core_y, right=right if mask + 1 in early else None)
        part = last_for(came[mask], core_y, begin=swap(odd, 1, n))
        total.append(swap(part, mask, n) if mask else part)
    return sum(total[1:], total[0])


def solution(mesh):
    n = mesh.shape[AXIS]

    def shards(core_x, core_y, left_intersection, right_intersection):
        rows = left_intersection.shape[1]
        fits = n >= 4 and n & (n - 1) == 0 and rows % 16 == 0 and core_x.shape[1] % 8 == 0 and core_x.shape[3] % LANES == 0
        if not fits:
            return plain(core_x, core_y, left_intersection, right_intersection)
        return exchanged(core_x, core_y, left_intersection, right_intersection, n)

    return jax.shard_map(
        shards,
        mesh=mesh,
        in_specs=(
            P("node", AXIS, None, None),
            P("node", AXIS, None, None),
            P("node", AXIS, None),
            P("node", AXIS, None),
        ),
        out_specs=P("node", AXIS, None),
        check_vma=False,
    )
```

```python
import functools

import jax
import jax.numpy as jnp
from jax import lax
from jax.experimental import pallas as pl
from jax.experimental.pallas import tpu as pltpu
from jax.sharding import PartitionSpec as P

AXIS = "cuts"
LIMIT = 20 * 1024 * 1024
MOST = 44 * 1024 * 1024
LANES = 128


def plain(core_x, core_y, left_intersection, right_intersection):
    left_full = lax.all_gather(left_intersection, AXIS, axis=1, tiled=True)
    first = jnp.einsum(
        "pik,paij->pakj", left_full, core_x, preferred_element_type=jnp.float32
    ).astype(jnp.bfloat16)
    right_full = lax.all_gather(right_intersection, AXIS, axis=1, tiled=True)
    moved = lax.all_to_all(
        jnp.einsum("pakj,pjl->pakl", first, right_full, preferred_element_type=jnp.float32).astype(
            jnp.bfloat16
        ),
        AXIS,
        split_axis=2,
        concat_axis=1,
        tiled=True,
    )
    mine = lax.psum_scatter(
        jnp.einsum("pakl,pklb->apb", moved, core_y, preferred_element_type=jnp.float32),
        AXIS,
        scatter_dimension=0,
        tiled=True,
    )
    return jnp.transpose(mine, (1, 0, 2))


def swap(value, mask, n):
    return lax.ppermute(value, AXIS, [(i, i ^ mask) for i in range(n)])


def packed(left, right):
    rows = left.shape[1]
    return jnp.pad(left, ((0, 0), (0, rows), (0, 0))) + jnp.pad(right, ((0, 0), (rows, 0), (0, 0)))


def gather_rows(value, n):
    even = {mask: swap(value, mask, n) for mask in range(n - 2, 0, -2)}
    even[0] = value
    rows = [None] * n
    for mask, came in even.items():
        rows[mask], rows[mask + 1] = came, swap(came, 1, n)
    return rows


def at_rows(me, mask, rows):
    return pl.ds(pl.multiple_of((me ^ mask) * rows, rows), rows)


def choose(me, masks, pieces, full, turned, chosen):
    rows = chosen.shape[0] // len(masks)
    for m, piece in enumerate(pieces):
        full[at_rows(me, m, rows), :] = piece[0, :rows]
    turned[...] = full[...].T
    for slot, m in enumerate(masks):
        chosen[slot * rows : (slot + 1) * rows, :] = turned[at_rows(me, m, rows), :]


def apply_right(first, right, second, flat_ref, count, rows):
    width = right.shape[1]
    whole = jnp.dot(first, right, preferred_element_type=jnp.float32)
    for h in range(width // LANES):
        second[h] = whole[:, h * LANES : (h + 1) * LANES]
    for k in range(rows):
        for h in range(width // LANES):
            flat_ref[:, k * width + h * LANES : k * width + (h + 1) * LANES] = second[
                h, pl.ds(k, count, stride=rows), :
            ].astype(jnp.bfloat16)


def first_kernel(n, masks, me_ref, *refs):
    pieces, x_ref, outs = refs[:n], refs[n], refs[n + 1 : -5]
    full, turned, chosen, held, sems = refs[-5:]
    parent, chunk = pl.program_id(0), pl.program_id(1)
    parents, chunks = sems.shape
    step, rows = outs[0].shape[1], outs[0].shape[2]

    def copy(p, c):
        at = pl.ds(c * step, step)
        return pltpu.make_async_copy(x_ref.at[p, at], held.at[p, at], sems.at[p, c])

    @pl.when((parent == 0) & (chunk == 0))
    def _():
        for p in range(parents):
            for c in range(chunks):
                copy(p, c).start()

    @pl.when(chunk == 0)
    def _():
        choose(me_ref[0], masks, pieces, full, turned, chosen)

    copy(parent, chunk).wait()
    for a in range(step):
        product = jnp.dot(
            chosen[...], held[parent, chunk * step + a], preferred_element_type=jnp.float32
        ).astype(jnp.bfloat16)
        for slot, out in enumerate(outs):
            out[0, a] = product[slot * rows : (slot + 1) * rows, :]


def first_for(me, pieces, core_x, masks):
    n = len(pieces)
    parents, mine, left, right = core_x.shape
    rows = left // n
    step = min(8, mine)
    return pl.pallas_call(
        functools.partial(first_kernel, n, masks),
        grid=(parents, mine // step),
        in_specs=[pl.BlockSpec(memory_space=pltpu.SMEM)]
        + [pl.BlockSpec((1, 2 * rows, left), lambda p, c: (p, 0, 0))] * n
        + [pl.BlockSpec(memory_space=pl.ANY)],
        out_specs=[pl.BlockSpec((1, step, rows, right), lambda p, c: (p, c, 0, 0))] * len(masks),
        out_shape=[jax.ShapeDtypeStruct((parents, mine, rows, right), jnp.bfloat16)] * len(masks),
        scratch_shapes=[
            pltpu.VMEM((left, left), jnp.bfloat16),
            pltpu.VMEM((left, left), jnp.bfloat16),
            pltpu.VMEM((rows * len(masks), left), jnp.bfloat16),
            pltpu.VMEM(core_x.shape, jnp.bfloat16),
            pltpu.SemaphoreType.DMA((parents, mine // step)),
        ],
        compiler_params=pltpu.CompilerParams(vmem_limit_bytes=MOST),
        cost_estimate=pl.CostEstimate(
            flops=2 * parents * mine * rows * len(masks) * left * right,
            bytes_accessed=2 * parents * mine * right * (left + rows * len(masks)),
            transcendentals=0,
        ),
        name="first",
    )(me, *pieces, core_x)


def second_kernel(n, masks, me_ref, *refs):
    pieces, x_ref = refs[:n], refs[n]
    outs, (full, turned, chosen, first, second) = refs[n + 2 : -5], refs[-5:]
    parent = pl.program_id(0)
    mine, rows = outs[0].shape[1], pieces[0].shape[1] // 2
    choose(me_ref[0], masks, pieces, full, turned, chosen)
    for m, piece in enumerate(pieces):
        full[at_rows(me_ref[0], m, rows), :] = piece[0, rows:]
    for a in range(mine):
        product = jnp.dot(chosen[...], x_ref[parent, a], preferred_element_type=jnp.float32).astype(jnp.bfloat16)
        for slot in range(len(masks)):
            first[slot, a * rows : (a + 1) * rows, :] = product[slot * rows : (slot + 1) * rows, :]
    for slot in range(len(masks)):
        if len(outs) == len(masks) or slot < len(masks) - 1:
            apply_right(first[slot], full[...], second, outs[slot].at[0], mine, rows)
        else:
            for p, out in enumerate(outs[slot:]):

                @pl.when(parent == p)
                def _(slot=slot, out=out):
                    apply_right(first[slot], full[...], second, out.at[0], mine, rows)


def second_for(me, pieces, core_x, masks, after, split=False):
    n = len(pieces)
    parents, mine, left, right = core_x.shape
    rows = left // n
    wide = rows * right
    whole = len(masks) - split
    return pl.pallas_call(
        functools.partial(second_kernel, n, masks),
        grid=(parents,),
        in_specs=[pl.BlockSpec(memory_space=pltpu.SMEM)]
        + [pl.BlockSpec((1, 2 * rows, left), lambda p: (p, 0, 0))] * n
        + [pl.BlockSpec(memory_space=pltpu.VMEM), pl.BlockSpec(memory_space=pl.ANY)],
        out_specs=[pl.BlockSpec((1, mine, wide), lambda p: (p, 0, 0))] * whole
        + [pl.BlockSpec((1, mine, wide), lambda p: (0, 0, 0))] * (parents * split),
        out_shape=[jax.ShapeDtypeStruct((parents, mine, wide), jnp.bfloat16)] * whole
        + [jax.ShapeDtypeStruct((1, mine, wide), jnp.bfloat16)] * (parents * split),
        scratch_shapes=[
            pltpu.VMEM((left, left), jnp.bfloat16),
            pltpu.VMEM((left, left), jnp.bfloat16),
            pltpu.VMEM((rows * len(masks), left), jnp.bfloat16),
            pltpu.VMEM((len(masks), mine * rows, right), jnp.bfloat16),
            pltpu.VMEM((right // LANES, mine * rows, LANES), jnp.float32),
        ],
        compiler_params=pltpu.CompilerParams(vmem_limit_bytes=LIMIT),
        cost_estimate=pl.CostEstimate(
            flops=2 * parents * mine * rows * len(masks) * right * (left + right),
            bytes_accessed=2 * parents * mine * right * (left + rows * len(masks)),
            transcendentals=0,
        ),
        name="second",
    )(me, *pieces, core_x, after)


def join_kernel(n, me_ref, *refs):
    pieces, out = refs[:n], refs[n]
    rows = pieces[0].shape[1] // 2
    for m in range(n):
        out[:, at_rows(me_ref[0], m, rows), :] = pieces[m][:, rows:]


def join_right(me, pieces):
    n = len(pieces)
    parents, rows, width = pieces[0].shape
    return pl.pallas_call(
        functools.partial(join_kernel, n),
        in_specs=[pl.BlockSpec(memory_space=pltpu.SMEM)] + [pl.BlockSpec(memory_space=pltpu.VMEM)] * n,
        out_specs=pl.BlockSpec(memory_space=pltpu.VMEM),
        out_shape=jax.ShapeDtypeStruct((parents, n * rows // 2, width), pieces[0].dtype),
        compiler_params=pltpu.CompilerParams(vmem_limit_bytes=LIMIT),
        cost_estimate=pl.CostEstimate(flops=0, bytes_accessed=2 * parents * n * rows * width, transcendentals=0),
        name="join",
    )(me, *pieces)


def last_kernel(parents, held, only, right_given, came, *refs):
    refs = list(refs)
    given, y_ref = [refs.pop(0) for _ in range(came)], refs.pop(0)
    begin_ref = refs.pop(0) if held else None
    right_ref = refs.pop(0) if right_given else None
    out_ref = refs.pop(0)
    depth = y_ref.shape[1] * y_ref.shape[2]
    wide = [(ref, i) for ref in given for i in range(ref.shape[0])]
    for slot in range(parents):
        parent = slot if only is None else only
        ref, i = wide[slot]
        if right_given:
            second, flat = refs
            _, count, rows, right = ref.shape
            apply_right(ref[i].reshape(count * rows, right), right_ref[parent], second, flat, count, rows)
            ref, i = flat, Ellipsis
        total = jnp.dot(ref[i], y_ref[parent].reshape(depth, y_ref.shape[3]), preferred_element_type=jnp.float32)
        out_ref[slot] = total + begin_ref[parent] if held else total


def last_for(came, core_y, begin=None, right=None, only=None):
    total, rows, width, out_width = core_y.shape
    parents, count = total if only is None else 1, came[0].shape[1]
    given = came + [core_y] + [x for x in (begin, right) if x is not None]
    whole = pl.BlockSpec(memory_space=pltpu.VMEM)
    scratch = []
    if right is not None:
        scratch = [
            pltpu.VMEM((width // LANES, count * rows, LANES), jnp.float32),
            pltpu.VMEM((count, rows * width), jnp.bfloat16),
        ]
    return pl.pallas_call(
        functools.partial(last_kernel, parents, begin is not None, only, right is not None, len(came)),
        in_specs=[whole] * len(given),
        out_specs=whole,
        out_shape=jax.ShapeDtypeStruct((parents, count, out_width), jnp.float32),
        scratch_shapes=scratch,
        compiler_params=pltpu.CompilerParams(vmem_limit_bytes=LIMIT),
        cost_estimate=pl.CostEstimate(
            flops=2 * parents * count * rows * width * (out_width + (width if scratch else 0)),
            bytes_accessed=2 * parents * rows * width * (count + out_width),
            transcendentals=0,
        ),
        name="last",
    )(*given)


def sum_kernel(parents, *refs):
    out_ref = refs[-1]
    for p in range(parents):
        total = refs[0][p]
        for ref in refs[1 : -1 - parents]:
            total += ref[p]
        out_ref[p] = total + refs[p - 1 - parents][0]


def summed(whole, cut):
    return pl.pallas_call(
        functools.partial(sum_kernel, len(cut)),
        in_specs=[pl.BlockSpec(memory_space=pltpu.VMEM)] * (len(whole) + len(cut)),
        out_specs=pl.BlockSpec(memory_space=pltpu.VMEM),
        out_shape=jax.ShapeDtypeStruct(whole[0].shape, whole[0].dtype),
        compiler_params=pltpu.CompilerParams(vmem_limit_bytes=LIMIT),
        cost_estimate=pl.CostEstimate(flops=whole[0].size, bytes_accessed=8 * whole[0].size, transcendentals=0),
        name="sum",
    )(*whole, *cut)


def exchanged(core_x, core_y, left_intersection, right_intersection, n):
    me = lax.axis_index(AXIS).astype(jnp.int32).reshape(1)
    parents = core_x.shape[0]
    pairs = list(range(2, n, 2))
    pieces = gather_rows(packed(left_intersection, right_intersection), n)
    early = [mask + 1 for mask in pairs[:2]]
    made = first_for(me, pieces, core_x, early)
    came = {mask: [swap(part, mask, n)] for mask, part in zip(early, made)}
    after = made[0]
    end = pairs[-1]
    for masks in [pairs[:2]] + [[mask + 1, mask] for mask in pairs[2:]] + [[1, 0]]:
        made = second_for(me, pieces, core_x, masks, after, end in masks)
        after = made[0]
        for mask in masks:
            if mask == end:
                came[mask] = [swap(part, mask, n) for part in made[-parents:]]
            else:
                part = made[masks.index(mask)]
                came[mask] = [swap(part, mask, n) if mask else part]
    right = join_right(me, pieces)
    whole, cut = [], []
    for mask in [0] + pairs:
        odd = swap(last_for(came[mask + 1], core_y, right=right if mask + 1 in early else None), 1, n)
        if mask == end:
            cut = [swap(last_for([came[mask][p]], core_y, odd, only=p), mask, n) for p in range(parents)]
        else:
            part = last_for(came[mask], core_y, odd)
            whole.append(swap(part, mask, n) if mask else part)
    return summed(whole, cut)


def solution(mesh):
    n = mesh.shape[AXIS]

    def shards(core_x, core_y, left_intersection, right_intersection):
        rows = left_intersection.shape[1]
        fits = n >= 4 and n & (n - 1) == 0 and rows % 16 == 0 and core_x.shape[1] % 8 == 0 and core_x.shape[3] % LANES == 0
        if not fits:
            return plain(core_x, core_y, left_intersection, right_intersection)
        return exchanged(core_x, core_y, left_intersection, right_intersection, n)

    return jax.shard_map(
        shards,
        mesh=mesh,
        in_specs=(
            P("node", AXIS, None, None),
            P("node", AXIS, None, None),
            P("node", AXIS, None),
            P("node", AXIS, None),
        ),
        out_specs=P("node", AXIS, None),
        check_vma=False,
    )
```

```python
import functools

import jax
import jax.numpy as jnp
from jax import lax
from jax.experimental import pallas as pl
from jax.experimental.pallas import tpu as pltpu
from jax.sharding import PartitionSpec as P

AXIS = "cuts"
LIMIT = 20 * 1024 * 1024
MOST = 44 * 1024 * 1024
LANES = 128


def plain(core_x, core_y, left_intersection, right_intersection):
    left_full = lax.all_gather(left_intersection, AXIS, axis=1, tiled=True)
    first = jnp.einsum(
        "pik,paij->pakj", left_full, core_x, preferred_element_type=jnp.float32
    ).astype(jnp.bfloat16)
    right_full = lax.all_gather(right_intersection, AXIS, axis=1, tiled=True)
    moved = lax.all_to_all(
        jnp.einsum("pakj,pjl->pakl", first, right_full, preferred_element_type=jnp.float32).astype(
            jnp.bfloat16
        ),
        AXIS,
        split_axis=2,
        concat_axis=1,
        tiled=True,
    )
    mine = lax.psum_scatter(
        jnp.einsum("pakl,pklb->apb", moved, core_y, preferred_element_type=jnp.float32),
        AXIS,
        scatter_dimension=0,
        tiled=True,
    )
    return jnp.transpose(mine, (1, 0, 2))


def swap(value, mask, n):
    return lax.ppermute(value, AXIS, [(i, i ^ mask) for i in range(n)])


def packed(left, right):
    rows = left.shape[1]
    return jnp.pad(left, ((0, 0), (0, rows), (0, 0))) + jnp.pad(right, ((0, 0), (rows, 0), (0, 0)))


def gather_rows(value, n):
    even = {mask: swap(value, mask, n) for mask in range(n - 2, 0, -2)}
    even[0] = value
    rows = [None] * n
    for mask, came in even.items():
        rows[mask], rows[mask + 1] = came, swap(came, 1, n)
    return rows


def at_rows(me, mask, rows):
    return pl.ds(pl.multiple_of((me ^ mask) * rows, rows), rows)


def choose(me, masks, pieces, full, turned, chosen):
    rows = chosen.shape[0] // len(masks)
    for m, piece in enumerate(pieces):
        full[at_rows(me, m, rows), :] = piece[0, :rows]
    turned[...] = full[...].T
    for slot, m in enumerate(masks):
        chosen[slot * rows : (slot + 1) * rows, :] = turned[at_rows(me, m, rows), :]


def apply_right(first, right, second, flat_ref, count, rows):
    width = right.shape[1]
    whole = jnp.dot(first, right, preferred_element_type=jnp.float32)
    for h in range(width // LANES):
        second[h] = whole[:, h * LANES : (h + 1) * LANES]
    for k in range(rows):
        for h in range(width // LANES):
            flat_ref[:, k * width + h * LANES : k * width + (h + 1) * LANES] = second[
                h, pl.ds(k, count, stride=rows), :
            ].astype(jnp.bfloat16)


def first_kernel(n, masks, me_ref, *refs):
    pieces, x_ref, outs = refs[:n], refs[n], refs[n + 1 : -5]
    full, turned, chosen, held, sems = refs[-5:]
    parent, chunk = pl.program_id(0), pl.program_id(1)
    parents, chunks = sems.shape
    step, rows = outs[0].shape[1], outs[0].shape[2]

    def copy(p, c):
        at = pl.ds(c * step, step)
        return pltpu.make_async_copy(x_ref.at[p, at], held.at[p, at], sems.at[p, c])

    @pl.when((parent == 0) & (chunk == 0))
    def _():
        for p in range(parents):
            for c in range(chunks):
                copy(p, c).start()

    @pl.when(chunk == 0)
    def _():
        choose(me_ref[0], masks, pieces, full, turned, chosen)

    copy(parent, chunk).wait()
    for a in range(step):
        product = jnp.dot(
            chosen[...], held[parent, chunk * step + a], preferred_element_type=jnp.float32
        ).astype(jnp.bfloat16)
        for slot, out in enumerate(outs):
            out[0, a] = product[slot * rows : (slot + 1) * rows, :]


def first_for(me, pieces, core_x, masks):
    n = len(pieces)
    parents, mine, left, right = core_x.shape
    rows = left // n
    step = min(8, mine)
    return pl.pallas_call(
        functools.partial(first_kernel, n, masks),
        grid=(parents, mine // step),
        in_specs=[pl.BlockSpec(memory_space=pltpu.SMEM)]
        + [pl.BlockSpec((1, 2 * rows, left), lambda p, c: (p, 0, 0))] * n
        + [pl.BlockSpec(memory_space=pl.ANY)],
        out_specs=[pl.BlockSpec((1, step, rows, right), lambda p, c: (p, c, 0, 0))] * len(masks),
        out_shape=[jax.ShapeDtypeStruct((parents, mine, rows, right), jnp.bfloat16)] * len(masks),
        scratch_shapes=[
            pltpu.VMEM((left, left), jnp.bfloat16),
            pltpu.VMEM((left, left), jnp.bfloat16),
            pltpu.VMEM((rows * len(masks), left), jnp.bfloat16),
            pltpu.VMEM(core_x.shape, jnp.bfloat16),
            pltpu.SemaphoreType.DMA((parents, mine // step)),
        ],
        compiler_params=pltpu.CompilerParams(vmem_limit_bytes=MOST),
        cost_estimate=pl.CostEstimate(
            flops=2 * parents * mine * rows * len(masks) * left * right,
            bytes_accessed=2 * parents * mine * right * (left + rows * len(masks)),
            transcendentals=0,
        ),
        name="first",
    )(me, *pieces, core_x)


def second_kernel(n, masks, me_ref, *refs):
    pieces, x_ref = refs[:n], refs[n]
    outs, (full, turned, chosen, first, second, right) = refs[n + 2 : -6], refs[-6:]
    parent = pl.program_id(0)
    mine, rows = outs[0].shape[1], pieces[0].shape[1] // 2
    choose(me_ref[0], masks, pieces, full, turned, chosen)
    for m, piece in enumerate(pieces):
        right[at_rows(me_ref[0], m, rows), :] = piece[0, rows:]
    for a in range(mine):
        product = jnp.dot(chosen[...], x_ref[parent, a], preferred_element_type=jnp.float32).astype(jnp.bfloat16)
        for slot in range(len(masks)):
            first[slot, a * rows : (a + 1) * rows, :] = product[slot * rows : (slot + 1) * rows, :]
    for slot in range(len(masks)):
        if len(outs) == len(masks) or slot < len(masks) - 1:
            apply_right(first[slot], right[...], second, outs[slot].at[0], mine, rows)
        else:
            for p, out in enumerate(outs[slot:]):

                @pl.when(parent == p)
                def _(slot=slot, out=out):
                    apply_right(first[slot], right[...], second, out.at[0], mine, rows)


def second_for(me, pieces, core_x, masks, after, split=False):
    n = len(pieces)
    parents, mine, left, right = core_x.shape
    rows = left // n
    wide = rows * right
    whole = len(masks) - split
    return pl.pallas_call(
        functools.partial(second_kernel, n, masks),
        grid=(parents,),
        in_specs=[pl.BlockSpec(memory_space=pltpu.SMEM)]
        + [pl.BlockSpec((1, 2 * rows, left), lambda p: (p, 0, 0))] * n
        + [pl.BlockSpec(memory_space=pltpu.VMEM), pl.BlockSpec(memory_space=pl.ANY)],
        out_specs=[pl.BlockSpec((1, mine, wide), lambda p: (p, 0, 0))] * whole
        + [pl.BlockSpec((1, mine, wide), lambda p: (0, 0, 0))] * (parents * split),
        out_shape=[jax.ShapeDtypeStruct((parents, mine, wide), jnp.bfloat16)] * whole
        + [jax.ShapeDtypeStruct((1, mine, wide), jnp.bfloat16)] * (parents * split),
        scratch_shapes=[
            pltpu.VMEM((left, left), jnp.bfloat16),
            pltpu.VMEM((left, left), jnp.bfloat16),
            pltpu.VMEM((rows * len(masks), left), jnp.bfloat16),
            pltpu.VMEM((len(masks), mine * rows, right), jnp.bfloat16),
            pltpu.VMEM((right // LANES, mine * rows, LANES), jnp.float32),
            pltpu.VMEM((right, right), jnp.bfloat16),
        ],
        compiler_params=pltpu.CompilerParams(vmem_limit_bytes=LIMIT),
        cost_estimate=pl.CostEstimate(
            flops=2 * parents * mine * rows * len(masks) * right * (left + right),
            bytes_accessed=2 * parents * mine * right * (left + rows * len(masks)),
            transcendentals=0,
        ),
        name="second",
    )(me, *pieces, core_x, after)


def join_kernel(n, me_ref, *refs):
    pieces, out = refs[:n], refs[n]
    rows = pieces[0].shape[1] // 2
    for m in range(n):
        out[:, at_rows(me_ref[0], m, rows), :] = pieces[m][:, rows:]


def join_right(me, pieces):
    n = len(pieces)
    parents, rows, width = pieces[0].shape
    return pl.pallas_call(
        functools.partial(join_kernel, n),
        in_specs=[pl.BlockSpec(memory_space=pltpu.SMEM)] + [pl.BlockSpec(memory_space=pltpu.VMEM)] * n,
        out_specs=pl.BlockSpec(memory_space=pltpu.VMEM),
        out_shape=jax.ShapeDtypeStruct((parents, n * rows // 2, width), pieces[0].dtype),
        compiler_params=pltpu.CompilerParams(vmem_limit_bytes=LIMIT),
        cost_estimate=pl.CostEstimate(flops=0, bytes_accessed=2 * parents * n * rows * width, transcendentals=0),
        name="join",
    )(me, *pieces)


def last_kernel(parents, held, only, right_given, came, *refs):
    refs = list(refs)
    given, y_ref = [refs.pop(0) for _ in range(came)], refs.pop(0)
    begin_ref = refs.pop(0) if held else None
    right_ref = refs.pop(0) if right_given else None
    out_ref = refs.pop(0)
    depth = y_ref.shape[1] * y_ref.shape[2]
    wide = [(ref, i) for ref in given for i in range(ref.shape[0])]
    for slot in range(parents):
        parent = slot if only is None else only
        ref, i = wide[slot]
        if right_given:
            second, flat = refs
            _, count, rows, right = ref.shape
            apply_right(ref[i].reshape(count * rows, right), right_ref[parent], second, flat, count, rows)
            ref, i = flat, Ellipsis
        total = jnp.dot(ref[i], y_ref[parent].reshape(depth, y_ref.shape[3]), preferred_element_type=jnp.float32)
        out_ref[slot] = total + begin_ref[parent] if held else total


def last_for(came, core_y, begin=None, right=None, only=None):
    total, rows, width, out_width = core_y.shape
    parents, count = total if only is None else 1, came[0].shape[1]
    given = came + [core_y] + [x for x in (begin, right) if x is not None]
    whole = pl.BlockSpec(memory_space=pltpu.VMEM)
    scratch = []
    if right is not None:
        scratch = [
            pltpu.VMEM((width // LANES, count * rows, LANES), jnp.float32),
            pltpu.VMEM((count, rows * width), jnp.bfloat16),
        ]
    return pl.pallas_call(
        functools.partial(last_kernel, parents, begin is not None, only, right is not None, len(came)),
        in_specs=[whole] * len(given),
        out_specs=whole,
        out_shape=jax.ShapeDtypeStruct((parents, count, out_width), jnp.float32),
        scratch_shapes=scratch,
        compiler_params=pltpu.CompilerParams(vmem_limit_bytes=LIMIT),
        cost_estimate=pl.CostEstimate(
            flops=2 * parents * count * rows * width * (out_width + (width if scratch else 0)),
            bytes_accessed=2 * parents * rows * width * (count + out_width),
            transcendentals=0,
        ),
        name="last",
    )(*given)


def sum_kernel(parents, *refs):
    out_ref = refs[-1]
    for p in range(parents):
        total = refs[0][p]
        for ref in refs[1 : -1 - parents]:
            total += ref[p]
        out_ref[p] = total + refs[p - 1 - parents][0]


def summed(whole, cut):
    return pl.pallas_call(
        functools.partial(sum_kernel, len(cut)),
        in_specs=[pl.BlockSpec(memory_space=pltpu.VMEM)] * (len(whole) + len(cut)),
        out_specs=pl.BlockSpec(memory_space=pltpu.VMEM),
        out_shape=jax.ShapeDtypeStruct(whole[0].shape, whole[0].dtype),
        compiler_params=pltpu.CompilerParams(vmem_limit_bytes=LIMIT),
        cost_estimate=pl.CostEstimate(flops=whole[0].size, bytes_accessed=8 * whole[0].size, transcendentals=0),
        name="sum",
    )(*whole, *cut)


def exchanged(core_x, core_y, left_intersection, right_intersection, n):
    me = lax.axis_index(AXIS).astype(jnp.int32).reshape(1)
    parents = core_x.shape[0]
    pairs = list(range(2, n, 2))
    pieces = gather_rows(packed(left_intersection, right_intersection), n)
    early = [mask + 1 for mask in pairs[:2]]
    made = first_for(me, pieces, core_x, early)
    came = {mask: [swap(part, mask, n)] for mask, part in zip(early, made)}
    after = made[0]
    end = pairs[-1]
    for masks in [pairs[:2]] + [[mask + 1, mask] for mask in pairs[2:]] + [[1, 0]]:
        made = second_for(me, pieces, core_x, masks, after, end in masks)
        after = made[0]
        for mask in masks:
            if mask == end:
                came[mask] = [swap(part, mask, n) for part in made[-parents:]]
            else:
                part = made[masks.index(mask)]
                came[mask] = [swap(part, mask, n) if mask else part]
    right = join_right(me, pieces)
    whole, cut = [], []
    for mask in [0] + pairs:
        odd = swap(last_for(came[mask + 1], core_y, right=right if mask + 1 in early else None), 1, n)
        if mask == end:
            cut = [swap(last_for([came[mask][p]], core_y, odd, only=p), mask, n) for p in range(parents)]
        else:
            part = last_for(came[mask], core_y, odd)
            whole.append(swap(part, mask, n) if mask else part)
    return summed(whole, cut)


def solution(mesh):
    n = mesh.shape[AXIS]

    def shards(core_x, core_y, left_intersection, right_intersection):
        rows = left_intersection.shape[1]
        fits = n >= 4 and n & (n - 1) == 0 and rows % 16 == 0 and core_x.shape[1] % 8 == 0 and core_x.shape[3] % LANES == 0
        if not fits:
            return plain(core_x, core_y, left_intersection, right_intersection)
        return exchanged(core_x, core_y, left_intersection, right_intersection, n)

    return jax.shard_map(
        shards,
        mesh=mesh,
        in_specs=(
            P("node", AXIS, None, None),
            P("node", AXIS, None, None),
            P("node", AXIS, None),
            P("node", AXIS, None),
        ),
        out_specs=P("node", AXIS, None),
        check_vma=False,
    )
```

```python
import functools

import jax
import jax.numpy as jnp
from jax import lax
from jax.experimental import pallas as pl
from jax.experimental.pallas import tpu as pltpu
from jax.sharding import PartitionSpec as P

AXIS = "cuts"
LIMIT = 20 * 1024 * 1024
MOST = 44 * 1024 * 1024
LANES = 128


def plain(core_x, core_y, left_intersection, right_intersection):
    left_full = lax.all_gather(left_intersection, AXIS, axis=1, tiled=True)
    first = jnp.einsum(
        "pik,paij->pakj", left_full, core_x, preferred_element_type=jnp.float32
    ).astype(jnp.bfloat16)
    right_full = lax.all_gather(right_intersection, AXIS, axis=1, tiled=True)
    moved = lax.all_to_all(
        jnp.einsum("pakj,pjl->pakl", first, right_full, preferred_element_type=jnp.float32).astype(
            jnp.bfloat16
        ),
        AXIS,
        split_axis=2,
        concat_axis=1,
        tiled=True,
    )
    mine = lax.psum_scatter(
        jnp.einsum("pakl,pklb->apb", moved, core_y, preferred_element_type=jnp.float32),
        AXIS,
        scatter_dimension=0,
        tiled=True,
    )
    return jnp.transpose(mine, (1, 0, 2))


def swap(value, mask, n):
    return lax.ppermute(value, AXIS, [(i, i ^ mask) for i in range(n)])


def packed(left, right):
    rows = left.shape[1]
    return jnp.pad(left, ((0, 0), (0, rows), (0, 0))) + jnp.pad(right, ((0, 0), (rows, 0), (0, 0)))


def gather_rows(value, n):
    even = {mask: swap(value, mask, n) for mask in range(n - 2, 0, -2)}
    even[0] = value
    rows = [None] * n
    for mask, came in even.items():
        rows[mask], rows[mask + 1] = came, swap(came, 1, n)
    return rows


def at_rows(me, mask, rows):
    return pl.ds(pl.multiple_of((me ^ mask) * rows, rows), rows)


def choose(me, masks, pieces, full, turned, chosen):
    rows = chosen.shape[0] // len(masks)
    for m, piece in enumerate(pieces):
        full[at_rows(me, m, rows), :] = piece[0, :rows]
    turned[...] = full[...].T
    for slot, m in enumerate(masks):
        chosen[slot * rows : (slot + 1) * rows, :] = turned[at_rows(me, m, rows), :]


def apply_right(first, right, second, flat_ref, count, rows):
    width = right.shape[1]
    whole = jnp.dot(first, right, preferred_element_type=jnp.float32)
    for h in range(width // LANES):
        second[h] = whole[:, h * LANES : (h + 1) * LANES]
    for k in range(rows):
        for h in range(width // LANES):
            flat_ref[:, k * width + h * LANES : k * width + (h + 1) * LANES] = second[
                h, pl.ds(k, count, stride=rows), :
            ].astype(jnp.bfloat16)


def first_kernel(n, masks, me_ref, *refs):
    pieces, x_ref, outs = refs[:n], refs[n], refs[n + 1 : -5]
    full, turned, chosen, held, sems = refs[-5:]
    parent, chunk = pl.program_id(0), pl.program_id(1)
    parents, chunks = sems.shape
    step, rows = outs[0].shape[1], outs[0].shape[2]

    def copy(p, c):
        at = pl.ds(c * step, step)
        return pltpu.make_async_copy(x_ref.at[p, at], held.at[p, at], sems.at[p, c])

    @pl.when((parent == 0) & (chunk == 0))
    def _():
        for p in range(parents):
            for c in range(chunks):
                copy(p, c).start()

    @pl.when(chunk == 0)
    def _():
        choose(me_ref[0], masks, pieces, full, turned, chosen)

    copy(parent, chunk).wait()
    for a in range(step):
        product = jnp.dot(
            chosen[...], held[parent, chunk * step + a], preferred_element_type=jnp.float32
        ).astype(jnp.bfloat16)
        for slot, out in enumerate(outs):
            out[0, a] = product[slot * rows : (slot + 1) * rows, :]


def first_for(me, pieces, core_x, masks):
    n = len(pieces)
    parents, mine, left, right = core_x.shape
    rows = left // n
    step = 16 if mine % 16 == 0 else min(8, mine)
    return pl.pallas_call(
        functools.partial(first_kernel, n, masks),
        grid=(parents, mine // step),
        in_specs=[pl.BlockSpec(memory_space=pltpu.SMEM)]
        + [pl.BlockSpec((1, 2 * rows, left), lambda p, c: (p, 0, 0))] * n
        + [pl.BlockSpec(memory_space=pl.ANY)],
        out_specs=[pl.BlockSpec((1, step, rows, right), lambda p, c: (p, c, 0, 0))] * len(masks),
        out_shape=[jax.ShapeDtypeStruct((parents, mine, rows, right), jnp.bfloat16)] * len(masks),
        scratch_shapes=[
            pltpu.VMEM((left, left), jnp.bfloat16),
            pltpu.VMEM((left, left), jnp.bfloat16),
            pltpu.VMEM((rows * len(masks), left), jnp.bfloat16),
            pltpu.VMEM(core_x.shape, jnp.bfloat16),
            pltpu.SemaphoreType.DMA((parents, mine // step)),
        ],
        compiler_params=pltpu.CompilerParams(vmem_limit_bytes=MOST),
        cost_estimate=pl.CostEstimate(
            flops=2 * parents * mine * rows * len(masks) * left * right,
            bytes_accessed=2 * parents * mine * right * (left + rows * len(masks)),
            transcendentals=0,
        ),
        name="first",
    )(me, *pieces, core_x)


def second_kernel(n, masks, me_ref, *refs):
    pieces, x_ref = refs[:n], refs[n]
    outs, (full, turned, chosen, first, second, right) = refs[n + 2 : -6], refs[-6:]
    parent = pl.program_id(0)
    mine, rows = outs[0].shape[1], pieces[0].shape[1] // 2
    choose(me_ref[0], masks, pieces, full, turned, chosen)
    for m, piece in enumerate(pieces):
        right[at_rows(me_ref[0], m, rows), :] = piece[0, rows:]
    for a in range(mine):
        product = jnp.dot(chosen[...], x_ref[parent, a], preferred_element_type=jnp.float32).astype(jnp.bfloat16)
        for slot in range(len(masks)):
            first[slot, a * rows : (a + 1) * rows, :] = product[slot * rows : (slot + 1) * rows, :]
    for slot in range(len(masks)):
        if len(outs) == len(masks) or slot < len(masks) - 1:
            apply_right(first[slot], right[...], second, outs[slot].at[0], mine, rows)
        else:
            for p, out in enumerate(outs[slot:]):

                @pl.when(parent == p)
                def _(slot=slot, out=out):
                    apply_right(first[slot], right[...], second, out.at[0], mine, rows)


def second_for(me, pieces, core_x, masks, after, split=False):
    n = len(pieces)
    parents, mine, left, right = core_x.shape
    rows = left // n
    wide = rows * right
    whole = len(masks) - split
    return pl.pallas_call(
        functools.partial(second_kernel, n, masks),
        grid=(parents,),
        in_specs=[pl.BlockSpec(memory_space=pltpu.SMEM)]
        + [pl.BlockSpec((1, 2 * rows, left), lambda p: (p, 0, 0))] * n
        + [pl.BlockSpec(memory_space=pltpu.VMEM), pl.BlockSpec(memory_space=pl.ANY)],
        out_specs=[pl.BlockSpec((1, mine, wide), lambda p: (p, 0, 0))] * whole
        + [pl.BlockSpec((1, mine, wide), lambda p: (0, 0, 0))] * (parents * split),
        out_shape=[jax.ShapeDtypeStruct((parents, mine, wide), jnp.bfloat16)] * whole
        + [jax.ShapeDtypeStruct((1, mine, wide), jnp.bfloat16)] * (parents * split),
        scratch_shapes=[
            pltpu.VMEM((left, left), jnp.bfloat16),
            pltpu.VMEM((left, left), jnp.bfloat16),
            pltpu.VMEM((rows * len(masks), left), jnp.bfloat16),
            pltpu.VMEM((len(masks), mine * rows, right), jnp.bfloat16),
            pltpu.VMEM((right // LANES, mine * rows, LANES), jnp.float32),
            pltpu.VMEM((right, right), jnp.bfloat16),
        ],
        compiler_params=pltpu.CompilerParams(vmem_limit_bytes=LIMIT),
        cost_estimate=pl.CostEstimate(
            flops=2 * parents * mine * rows * len(masks) * right * (left + right),
            bytes_accessed=2 * parents * mine * right * (left + rows * len(masks)),
            transcendentals=0,
        ),
        name="second",
    )(me, *pieces, core_x, after)


def join_kernel(n, me_ref, *refs):
    pieces, out = refs[:n], refs[n]
    rows = pieces[0].shape[1] // 2
    for m in range(n):
        out[:, at_rows(me_ref[0], m, rows), :] = pieces[m][:, rows:]


def join_right(me, pieces):
    n = len(pieces)
    parents, rows, width = pieces[0].shape
    return pl.pallas_call(
        functools.partial(join_kernel, n),
        in_specs=[pl.BlockSpec(memory_space=pltpu.SMEM)] + [pl.BlockSpec(memory_space=pltpu.VMEM)] * n,
        out_specs=pl.BlockSpec(memory_space=pltpu.VMEM),
        out_shape=jax.ShapeDtypeStruct((parents, n * rows // 2, width), pieces[0].dtype),
        compiler_params=pltpu.CompilerParams(vmem_limit_bytes=LIMIT),
        cost_estimate=pl.CostEstimate(flops=0, bytes_accessed=2 * parents * n * rows * width, transcendentals=0),
        name="join",
    )(me, *pieces)


def last_kernel(parents, held, only, right_given, came, *refs):
    refs = list(refs)
    given, y_ref = [refs.pop(0) for _ in range(came)], refs.pop(0)
    begin_ref = refs.pop(0) if held else None
    right_ref = refs.pop(0) if right_given else None
    out_ref = refs.pop(0)
    depth = y_ref.shape[1] * y_ref.shape[2]
    wide = [(ref, i) for ref in given for i in range(ref.shape[0])]
    for slot in range(parents):
        parent = slot if only is None else only
        ref, i = wide[slot]
        if right_given:
            second, flat = refs
            _, count, rows, right = ref.shape
            apply_right(ref[i].reshape(count * rows, right), right_ref[parent], second, flat, count, rows)
            ref, i = flat, Ellipsis
        total = jnp.dot(ref[i], y_ref[parent].reshape(depth, y_ref.shape[3]), preferred_element_type=jnp.float32)
        out_ref[slot] = total + begin_ref[parent] if held else total


def last_for(came, core_y, begin=None, right=None, only=None):
    total, rows, width, out_width = core_y.shape
    parents, count = total if only is None else 1, came[0].shape[1]
    given = came + [core_y] + [x for x in (begin, right) if x is not None]
    whole = pl.BlockSpec(memory_space=pltpu.VMEM)
    scratch = []
    if right is not None:
        scratch = [
            pltpu.VMEM((width // LANES, count * rows, LANES), jnp.float32),
            pltpu.VMEM((count, rows * width), jnp.bfloat16),
        ]
    return pl.pallas_call(
        functools.partial(last_kernel, parents, begin is not None, only, right is not None, len(came)),
        in_specs=[whole] * len(given),
        out_specs=whole,
        out_shape=jax.ShapeDtypeStruct((parents, count, out_width), jnp.float32),
        scratch_shapes=scratch,
        compiler_params=pltpu.CompilerParams(vmem_limit_bytes=LIMIT),
        cost_estimate=pl.CostEstimate(
            flops=2 * parents * count * rows * width * (out_width + (width if scratch else 0)),
            bytes_accessed=2 * parents * rows * width * (count + out_width),
            transcendentals=0,
        ),
        name="last",
    )(*given)


def sum_kernel(parents, *refs):
    out_ref = refs[-1]
    for p in range(parents):
        total = refs[0][p]
        for ref in refs[1 : -1 - parents]:
            total += ref[p]
        out_ref[p] = total + refs[p - 1 - parents][0]


def summed(whole, cut):
    return pl.pallas_call(
        functools.partial(sum_kernel, len(cut)),
        in_specs=[pl.BlockSpec(memory_space=pltpu.VMEM)] * (len(whole) + len(cut)),
        out_specs=pl.BlockSpec(memory_space=pltpu.VMEM),
        out_shape=jax.ShapeDtypeStruct(whole[0].shape, whole[0].dtype),
        compiler_params=pltpu.CompilerParams(vmem_limit_bytes=LIMIT),
        cost_estimate=pl.CostEstimate(flops=whole[0].size, bytes_accessed=8 * whole[0].size, transcendentals=0),
        name="sum",
    )(*whole, *cut)


def exchanged(core_x, core_y, left_intersection, right_intersection, n):
    me = lax.axis_index(AXIS).astype(jnp.int32).reshape(1)
    parents = core_x.shape[0]
    pairs = list(range(2, n, 2))
    pieces = gather_rows(packed(left_intersection, right_intersection), n)
    early = [mask + 1 for mask in pairs[:2]]
    made = first_for(me, pieces, core_x, early)
    came = {mask: [swap(part, mask, n)] for mask, part in zip(early, made)}
    after = made[0]
    end = pairs[-1]
    for masks in [pairs[:2]] + [[mask + 1, mask] for mask in pairs[2:]] + [[1, 0]]:
        made = second_for(me, pieces, core_x, masks, after, end in masks)
        after = made[0]
        for mask in masks:
            if mask == end:
                came[mask] = [swap(part, mask, n) for part in made[-parents:]]
            else:
                part = made[masks.index(mask)]
                came[mask] = [swap(part, mask, n) if mask else part]
    right = join_right(me, pieces)
    whole, cut = [], []
    for mask in [0] + pairs:
        odd = swap(last_for(came[mask + 1], core_y, right=right if mask + 1 in early else None), 1, n)
        if mask == end:
            cut = [swap(last_for([came[mask][p]], core_y, odd, only=p), mask, n) for p in range(parents)]
        else:
            part = last_for(came[mask], core_y, odd)
            whole.append(swap(part, mask, n) if mask else part)
    return summed(whole, cut)


def solution(mesh):
    n = mesh.shape[AXIS]

    def shards(core_x, core_y, left_intersection, right_intersection):
        rows = left_intersection.shape[1]
        fits = n >= 4 and n & (n - 1) == 0 and rows % 16 == 0 and core_x.shape[1] % 8 == 0 and core_x.shape[3] % LANES == 0
        if not fits:
            return plain(core_x, core_y, left_intersection, right_intersection)
        return exchanged(core_x, core_y, left_intersection, right_intersection, n)

    return jax.shard_map(
        shards,
        mesh=mesh,
        in_specs=(
            P("node", AXIS, None, None),
            P("node", AXIS, None, None),
            P("node", AXIS, None),
            P("node", AXIS, None),
        ),
        out_specs=P("node", AXIS, None),
        check_vma=False,
    )
```
